32 devices in a mesh: tgt: 8 (over y, x, core), src: 4 (over z).
Axes of the slice: x: 2, y: 2, z: 4, core: 2. Of those that a mesh axis runs over, the one named last changes fastest.
Arguments:
- states_late: bfloat16 [8192, 128], P('src'), may hold values from -12 to 12
- offset_late: bfloat16 [8192], P('src'), may hold values from 0 to 2
- values_late: bfloat16 [8192, 64], P('src'), may hold values from -6 to 6
- states_mid: bfloat16 [8192, 128], P('tgt'), may hold values from -12 to 12
- offset_mid: bfloat16 [8192], P('src'), may hold values from 0 to 2
- exercise_mid: bfloat16 [8192, 64], P('tgt'), may hold values from -6 to 6
- mask_mid: int32 [16, 16], replicated, may hold values from 0 to 1, as said below
- states_early: bfloat16 [8192, 128], P('tgt'), may hold values from -12 to 12
- exercise_early: bfloat16 [8192, 64], P('tgt'), may hold values from -6 to 6
- mask_early: int32 [16, 16], replicated, may hold values from 0 to 1, as said below
Outputs:
- value_mid: bfloat16 [8192, 64], P('tgt')
- value_early: bfloat16 [8192, 64], P('tgt')
The draws below stay inside these ranges and needn't reach their ends.
Inputs may be any that keep to these rules, and one draw needn't show every extreme that they name: `mask_mid`: 1 marks a live tile of 512 x 512 paths; every diagonal tile is live. `mask_early`: 1 marks a live tile of 512 x 512 paths; every diagonal tile is live.
All inputs are finite; a program needn't handle non-finite values.
Results may differ from the reference program's by a relative error of at most 0.0055.
Values may be sent and summed in bfloat16 or wider, within the bound.
A program may use at most 64 MiB of HBM per device.

```python
import math
import jax
import jax.numpy as jnp
from jax import lax

K = 128
V = 64
BLOCK = 512
PATHS = 8192
NB = 16


def hot_signs(key):
    flips = jax.random.bernoulli(jax.random.fold_in(key, 99), 0.5, (K,))
    amplitude = math.sqrt(60.0) * K ** (-0.25)
    return jnp.where(flips, amplitude, -amplitude).astype(jnp.float32)


def state_draw(key, role):
    noise = jnp.clip(jax.random.normal(jax.random.fold_in(key, 11 + role), (PATHS, K), jnp.float32), -6.0, 6.0)
    signs = hot_signs(key)
    path_ids = jnp.arange(PATHS)
    block_ids = path_ids // BLOCK
    within = path_ids % BLOCK
    levels = jnp.array([0.8, 1.1, 1.4], jnp.float32)
    strength = levels[block_ids // 4 % 3]
    hot_block = block_ids % 4 == 0
    first = hot_block & (within == 1)
    second = hot_block & (within == 3) & (role > 0)
    gain = jnp.where(first, strength, jnp.where(second, strength - 0.01, 0.0))
    chosen = first | second
    noise = jnp.where(chosen[:, None], gain[:, None] * signs[None, :], noise)
    return noise.astype(jnp.bfloat16)


def tile_mask_draw(key, salt):
    rates = jax.random.randint(jax.random.fold_in(key, salt), (NB, 1), 2, 9)
    rolls = jax.random.randint(jax.random.fold_in(key, salt + 1), (NB, NB), 0, 8)
    diagonal = jnp.arange(NB)[:, None] == jnp.arange(NB)[None, :]
    return ((rolls < rates) | diagonal).astype(jnp.int32)


def draw_states_late(key, part):
    return state_draw(key, 2)


def draw_states_mid(key, part):
    return state_draw(key, 1)


def draw_states_early(key, part):
    return state_draw(key, 0)


def draw_mask_mid(key, part):
    return tile_mask_draw(key, 41)


def draw_mask_early(key, part):
    return tile_mask_draw(key, 51)


def block_levels(own_key, extent, split, least, high):
    level, own = 1.0, jax.random.fold_in(own_key, 6)
    for dim, shards_of in split:
        heights = jnp.exp(jax.random.uniform(jax.random.fold_in(own, dim), (shards_of,), jnp.float32, least / len(split), high / len(split)))
        level = level * jnp.repeat(heights, extent[dim] // shards_of).reshape([-1 if axis == dim else 1 for axis in range(len(extent))])
    return level


def bell_draw(rng, extent, width, most, cuts=(), dtype=jnp.bfloat16):
    drawn = width * jax.random.normal(rng, extent, jnp.float32)
    if cuts:
        drawn = drawn * block_levels(rng, extent, cuts, -0.22, 0.18)
    return jnp.clip(drawn, -most, most).astype(dtype)


def setup_inputs(seed: int = 0) -> dict:
    keys = jax.random.split(jax.random.key(seed), 11)
    return {
        "states_late": draw_states_late(jax.random.fold_in(keys[10], 71), 0),
        "offset_late": jnp.clip(2.0 * jax.random.uniform(keys[1], (PATHS,), jnp.float32) ** block_levels(keys[1], (PATHS,), ((0, 4),), -0.2, 0.2), 0.0, 2.0).astype(jnp.bfloat16),
        "values_late": bell_draw(keys[2], (PATHS, V), 1.0, 6.0, ((0, 4),)),
        "states_mid": draw_states_mid(jax.random.fold_in(keys[10], 71), 0),
        "offset_mid": jnp.clip(2.0 * jax.random.uniform(keys[4], (PATHS,), jnp.float32) ** block_levels(keys[4], (PATHS,), ((0, 4),), -0.2, 0.2), 0.0, 2.0).astype(jnp.bfloat16),
        "exercise_mid": bell_draw(keys[5], (PATHS, V), 0.4, 6.0, ((0, 8),)),
        "mask_mid": draw_mask_mid(jax.random.fold_in(keys[10], 71), 0),
        "states_early": draw_states_early(jax.random.fold_in(keys[10], 71), 0),
        "exercise_early": bell_draw(keys[8], (PATHS, V), 0.4, 6.0, ((0, 8),)),
        "mask_early": draw_mask_early(jax.random.fold_in(keys[10], 71), 0),
    }


sharpness = 3.5
very_low = -1.0e30


def date_values(targets, sources, offsets, values, tile_mask, exercise):
    score_scale = sharpness / (K ** 0.5)
    source_f = sources.astype(jnp.float32)
    offset_f = offsets.astype(jnp.float32)
    value_f = values.astype(jnp.float32)
    live_table = jnp.repeat(tile_mask, BLOCK, axis=1)
    target_blocks = targets.reshape(NB, BLOCK, K)
    exercise_blocks = exercise.reshape(NB, BLOCK, V)

    def block_values(inputs):
        target_rows, exercise_rows, live_row = inputs
        scores = jnp.dot(target_rows.astype(jnp.float32), source_f.T, precision=lax.Precision.HIGHEST)
        scores = scores * score_scale - offset_f[None, :]
        live_cols = (live_row > 0)[None, :]
        scores = jnp.where(live_cols, scores, very_low)
        row_peak = jnp.max(scores, axis=1)
        weights = jnp.where(live_cols, jnp.exp(scores - row_peak[:, None]), 0.0)
        weight_sum = jnp.sum(weights, axis=1)
        rounded = lax.optimization_barrier(weights.astype(jnp.bfloat16)).astype(jnp.float32)
        weighted = jnp.dot(rounded, value_f, precision=lax.Precision.HIGHEST)
        continuation = weighted / weight_sum[:, None]
        return jnp.maximum(continuation, exercise_rows.astype(jnp.float32)).astype(jnp.bfloat16)

    result = lax.map(block_values, (target_blocks, exercise_blocks, live_table))
    return result.reshape(PATHS, V)


def reference(states_late, offset_late, values_late, states_mid, offset_mid, exercise_mid, mask_mid, states_early, exercise_early, mask_early):
    value_mid = date_values(states_mid, states_late, offset_late, values_late, mask_mid, exercise_mid)
    value_early = date_values(states_early, states_mid, offset_mid, value_mid, mask_early, exercise_early)
    return (value_mid, value_early)
```

```python
import functools
import math

import jax
import jax.numpy as jnp
from jax import lax
from jax.experimental import pallas as pl
from jax.experimental.pallas import tpu as pltpu
from jax.sharding import PartitionSpec as P

BLOCK = 512
SHARPNESS = 3.5
LOG2E = math.log2(math.e)
DEAD = 1e30
MESH = pl.DeviceIdType.MESH


def eye(size):
    rows = lax.broadcasted_iota(jnp.int32, (size, size), 0)
    cols = lax.broadcasted_iota(jnp.int32, (size, size), 1)
    return rows == cols


def to_row(column):
    return jnp.sum(jnp.where(eye(column.shape[0]), column, 0.0), axis=0, keepdims=True)


def to_column(row):
    return jnp.sum(jnp.where(eye(row.shape[1]), row, 0.0), axis=1, keepdims=True)


def pack(rows):
    half = rows.shape[0] // 2
    return jnp.concatenate([rows[:half], rows[half:]], axis=1)


def kernel(
    n,
    x1_ref,
    y1_ref,
    h1_ref,
    w1_ref,
    h2_ref,
    e1_ref,
    m1_ref,
    x2_ref,
    e2_ref,
    m2_ref,
    out1_ref,
    out2_ref,
    states,
    offs,
    weights,
    scale2,
    peak_own,
    sum_own,
    acc_own,
    send_w,
    send_s,
    recv_w,
    recv_s,
    gathered,
    far,
    near,
    vals,
    early_pack,
    st_sem,
    off_sem,
    part_send,
    part_recv,
    gat_send,
    gat_recv,
    val_sem,
):
    t = lax.axis_index("tgt")
    s = lax.axis_index("src")
    chip = t // 2
    core = lax.rem(t, 2)
    mate = jnp.bitwise_xor(chip, s)
    partner = 2 * mate + core
    sibling = 2 * chip + 1 - core
    remote = s != 0
    rows_all, width = x1_ref.shape[0], w1_ref.shape[1]
    rows = rows_all // n
    half = rows // 2
    group = min(rows, 128)
    groups = rows // group
    cols = y1_ref.shape[0]
    part = cols // 2
    factor = SHARPNESS / math.sqrt(x1_ref.shape[1]) * LOG2E

    def peer(i):
        return lax.rem(s + i, n)

    barrier = pltpu.get_barrier_semaphore()
    for i in range(1, n):
        pl.semaphore_signal(barrier, inc=1, device_id=(t, peer(i)), device_id_type=MESH)
    pl.semaphore_signal(barrier, inc=1, device_id=(sibling, s), device_id_type=MESH)

    @pl.when(remote)
    def _():
        pl.semaphore_signal(barrier, inc=1, device_id=(partner, s), device_id_type=MESH)

    pl.semaphore_wait(barrier, jnp.where(remote, n + 1, n))

    states_far = pltpu.make_async_remote_copy(
        x1_ref, states.at[0], st_sem.at[0], st_sem.at[1], (partner, s), MESH
    )
    states_here = pltpu.make_async_copy(x1_ref, states.at[0], st_sem.at[0])
    states_near = pltpu.make_async_remote_copy(
        states.at[0], states.at[1], st_sem.at[2], st_sem.at[3], (sibling, s), MESH
    )
    offs_far = pltpu.make_async_remote_copy(h2_ref, offs, off_sem.at[0], off_sem.at[1], (t, mate), MESH)
    offs_here = pltpu.make_async_copy(h2_ref, offs, off_sem.at[0])

    @pl.when(remote)
    def _():
        states_far.start()

    @pl.when(jnp.logical_not(remote))
    def _():
        states_here.start()

    @pl.when(mate != s)
    def _():
        offs_far.start()

    @pl.when(mate == s)
    def _():
        offs_here.start()

    def bias(offset_row, mask_ref, row_tile, col_tile):
        tiles = []
        for c in range(offset_row.shape[1] // BLOCK):
            dead = jnp.where(mask_ref[row_tile, col_tile + c] > 0, 0.0, DEAD)
            tiles.append(offset_row[:, c * BLOCK : (c + 1) * BLOCK] * LOG2E + dead)
        return jnp.concatenate(tiles, axis=1)

    def scores(x, y, bias_row):
        dots = lax.dot_general(x, y, (((1,), (1,)), ((), ())), preferred_element_type=jnp.float32)
        return dots * factor - bias_row

    def part_copies(d, i):
        to = (t, peer(i))
        return (
            pltpu.make_async_remote_copy(
                send_w.at[d, i], recv_w.at[d, i], part_send.at[d, 0, i], part_recv.at[d, 0, i], to, MESH
            ),
            pltpu.make_async_remote_copy(
                send_s.at[d, i], recv_s.at[d, i], part_send.at[d, 1, i], part_recv.at[d, 1, i], to, MESH
            ),
        )

    def ship(d, i, peak, total, acc):
        send_w[d, i] = pack(acc.astype(jnp.bfloat16))
        for g in range(groups):
            send_s[d, i, g : g + 1, 0:group] = to_row(peak[g * group : (g + 1) * group])
            send_s[d, i, 4 + g : 5 + g, 0:group] = to_row(total[g * group : (g + 1) * group])
        for copy in part_copies(d, i):
            copy.start()

    def keep(peak, total, acc):
        peak_own[...] = peak
        sum_own[...] = total
        acc_own[...] = acc

    def combine(d, exercise_ref):
        for i in range(1, n):
            for copy in part_copies(d, i):
                copy.wait_recv()
        peaks, sums = [peak_own[...]], [sum_own[...]]
        for i in range(1, n):
            peaks.append(jnp.concatenate([to_column(recv_s[d, i, g : g + 1, 0:group]) for g in range(groups)], 0))
            sums.append(
                jnp.concatenate([to_column(recv_s[d, i, 4 + g : 5 + g, 0:group]) for g in range(groups)], 0)
            )
        top = functools.reduce(jnp.maximum, peaks)
        shrink = jnp.exp2(peaks[0] - top)
        total = sums[0] * shrink
        acc = acc_own[...] * shrink
        for i in range(1, n):
            shrink = jnp.exp2(peaks[i] - top)
            total = total + sums[i] * shrink
            packed = recv_w[d, i].astype(jnp.float32)
            acc = acc + jnp.concatenate([packed[:, :width], packed[:, width:]], 0) * shrink
        own = pl.ds(pl.multiple_of(s * rows, rows), rows)
        result = jnp.maximum(acc / total, exercise_ref[own, :].astype(jnp.float32))
        return pack(result.astype(jnp.bfloat16))

    def gather_copy(d, buffer, i, slot):
        return pltpu.make_async_remote_copy(
            buffer.at[slot], buffer.at[slot], gat_send.at[d, i], gat_recv.at[d, slot], (t, peer(i)), MESH
        )

    def unpack_to(ref, base, packed):
        ref[pl.ds(pl.multiple_of(base, rows), half), :] = packed[:, :width]
        ref[pl.ds(pl.multiple_of(base + half, half), half), :] = packed[:, width:]

    def first_date(i):
        q = peer(i)
        x = x1_ref[pl.ds(pl.multiple_of(q * rows, rows), rows), :]
        row_tile = (t * rows_all + q * rows) // BLOCK
        sc = scores(x, y1_ref[...], bias(h1_ref[...], m1_ref, row_tile, s * (cols // BLOCK)))
        peak = jnp.max(sc, axis=1, keepdims=True)
        w = jnp.exp2(sc - peak)
        total = jnp.sum(w, axis=1, keepdims=True)
        acc = jnp.dot(w.astype(jnp.bfloat16), w1_ref[...], preferred_element_type=jnp.float32)
        return peak, total, acc

    def first_step(i, carry):
        ship(0, i, *first_date(i))
        return carry

    lax.fori_loop(1, n, first_step, 0)
    keep(*first_date(0))

    @pl.when(remote)
    def _():
        states_far.wait()

    @pl.when(jnp.logical_not(remote))
    def _():
        states_here.wait()

    @pl.when(mate != s)
    def _():
        offs_far.wait()

    @pl.when(mate == s)
    def _():
        offs_here.wait()

    states_near.start()

    def second_weights(k):
        owner = 2 * mate + (core if k == 0 else 1 - core)
        offset_row = offs[:, pl.ds(pl.multiple_of((owner - 2 * mate) * part, part), part)]

        def step(q, carry):
            span = pl.ds(pl.multiple_of(q * rows, rows), rows)
            row_tile = (t * rows_all + q * rows) // BLOCK
            sc = scores(
                x2_ref[span, :],
                states[k],
                bias(offset_row, m2_ref, row_tile, owner * (part // BLOCK)),
            )
            peak = jnp.max(sc, axis=1, keepdims=True)
            w = jnp.exp2(sc - peak)
            weights[k, span, :] = w.astype(jnp.bfloat16)
            scale2[2 * k, span, :] = peak
            scale2[2 * k + 1, span, :] = jnp.sum(w, axis=1, keepdims=True)
            return carry

        lax.fori_loop(0, n, step, 0)

    second_weights(0)

    gathered[s] = combine(0, e1_ref)
    for i in range(1, n):
        gather_copy(0, gathered, i, s).start()

    def far_copy(q):
        return pltpu.make_async_remote_copy(
            gathered.at[q], far.at[q], val_sem.at[0, q], val_sem.at[1, q], (partner, s), MESH
        )

    def here_copy(q):
        return pltpu.make_async_copy(gathered.at[q], far.at[q], val_sem.at[0, q])

    def near_copy(q):
        return pltpu.make_async_remote_copy(
            far.at[q], near.at[q], val_sem.at[2, q], val_sem.at[3, q], (sibling, s), MESH
        )

    def pass_on(q):
        @pl.when(remote)
        def _():
            far_copy(q).start()

        @pl.when(jnp.logical_not(remote))
        def _():
            here_copy(q).start()

    pass_on(s)
    states_near.wait()
    second_weights(1)

    for i in range(1, n):
        gather_copy(0, gathered, i, peer(i)).wait_recv()
        pass_on(peer(i))

    for i in range(n):
        q = peer(i)

        @pl.when(remote)
        def _():
            far_copy(q).wait_recv()

        @pl.when(jnp.logical_not(remote))
        def _():
            here_copy(q).wait()

        near_copy(q).start()
        unpack_to(vals.at[0], q * rows, far[q])
    for i in range(n):
        q = peer(i)
        unpack_to(out1_ref, q * rows, gathered[q])
    for i in range(n):
        q = peer(i)
        near_copy(q).wait_recv()
        unpack_to(vals.at[1], q * rows, near[q])

    def second_date(i):
        span = pl.ds(pl.multiple_of(peer(i) * rows, rows), rows)
        peak0, peak1 = scale2[0, span, :], scale2[2, span, :]
        peak = jnp.maximum(peak0, peak1)
        f0, f1 = jnp.exp2(peak0 - peak), jnp.exp2(peak1 - peak)
        total = f0 * scale2[1, span, :] + f1 * scale2[3, span, :]
        acc = f0 * jnp.dot(weights[0, span, :], vals[0], preferred_element_type=jnp.float32)
        acc = acc + f1 * jnp.dot(weights[1, span, :], vals[1], preferred_element_type=jnp.float32)
        return peak, total, acc

    def second_step(i, carry):
        ship(1, i, *second_date(i))
        return carry

    lax.fori_loop(1, n, second_step, 0)
    keep(*second_date(0))

    early_pack[s] = combine(1, e2_ref)
    for i in range(1, n):
        gather_copy(1, early_pack, i, s).start()
    unpack_to(out2_ref, s * rows, early_pack[s])
    for i in range(1, n):
        q = peer(i)
        gather_copy(1, early_pack, i, q).wait_recv()
        unpack_to(out2_ref, q * rows, early_pack[q])

    for d in range(2):
        for i in range(1, n):
            for copy in part_copies(d, i):
                copy.wait_send()
            gather_copy(d, gathered if d == 0 else early_pack, i, s).wait_send()
    for q in range(n):
        near_copy(q).wait_send()

        @pl.when(remote)
        def _():
            far_copy(q).wait_send()


def per_device(n, states_late, offset_late, values_late, states_mid, offset_mid, exercise_mid, mask_mid,
               states_early, exercise_early, mask_early):
    rows_all, factors = states_mid.shape
    cols, width = values_late.shape
    rows = rows_all // n
    half = rows // 2
    part = cols // 2
    bf16, f32 = jnp.bfloat16, jnp.float32
    vmem = pl.BlockSpec(memory_space=pltpu.VMEM)
    smem = pl.BlockSpec(memory_space=pltpu.SMEM)
    pairs = 2 * rows_all * cols
    call = pl.pallas_call(
        functools.partial(kernel, n),
        out_shape=(
            jax.ShapeDtypeStruct((rows_all, width), bf16),
            jax.ShapeDtypeStruct((rows_all, width), bf16),
        ),
        in_specs=[vmem, vmem, vmem, vmem, vmem, vmem, smem, vmem, vmem, smem],
        out_specs=(vmem, vmem),
        scratch_shapes=[
            pltpu.VMEM((2, rows_all, factors), bf16),
            pltpu.VMEM((1, cols), f32),
            pltpu.VMEM((2, rows_all, part), bf16),
            pltpu.VMEM((4, rows_all, 1), f32),
            pltpu.VMEM((rows, 1), f32),
            pltpu.VMEM((rows, 1), f32),
            pltpu.VMEM((rows, width), f32),
            pltpu.VMEM((2, n, half, 2 * width), bf16),
            pltpu.VMEM((2, n, 8, 128), f32),
            pltpu.VMEM((2, n, half, 2 * width), bf16),
            pltpu.VMEM((2, n, 8, 128), f32),
            pltpu.VMEM((n, half, 2 * width), bf16),
            pltpu.VMEM((n, half, 2 * width), bf16),
            pltpu.VMEM((n, half, 2 * width), bf16),
            pltpu.VMEM((2, part, width), bf16),
            pltpu.VMEM((n, half, 2 * width), bf16),
            pltpu.SemaphoreType.DMA((4,)),
            pltpu.SemaphoreType.DMA((2,)),
            pltpu.SemaphoreType.DMA((2, 2, n)),
            pltpu.SemaphoreType.DMA((2, 2, n)),
            pltpu.SemaphoreType.DMA((2, n)),
            pltpu.SemaphoreType.DMA((2, n)),
            pltpu.SemaphoreType.DMA((4, n)),
        ],
        compiler_params=pltpu.CompilerParams(
            collective_id=0, has_side_effects=True, vmem_limit_bytes=48 * 1024 * 1024
        ),
        cost_estimate=pl.CostEstimate(
            flops=2 * pairs * (factors + width), bytes_accessed=4 * 1024 * 1024, transcendentals=pairs
        ),
    )
    return call(
        states_mid,
        states_late,
        offset_late.astype(f32).reshape(1, cols),
        values_late,
        offset_mid.astype(f32).reshape(1, cols),
        exercise_mid,
        mask_mid,
        states_early,
        exercise_early,
        mask_early,
    )


def solution(mesh):
    in_specs = (
        P("src", None),
        P("src"),
        P("src", None),
        P("tgt", None),
        P("src"),
        P("tgt", None),
        P(),
        P("tgt", None),
        P("tgt", None),
        P(),
    )
    out_specs = (P("tgt", None), P("tgt", None))
    return jax.shard_map(
        functools.partial(per_device, mesh.shape["src"]),
        mesh=mesh,
        in_specs=in_specs,
        out_specs=out_specs,
        check_vma=False,
    )
```

```python
import functools
import math

import jax
import jax.numpy as jnp
from jax import lax
from jax.experimental import pallas as pl
from jax.experimental.pallas import tpu as pltpu
from jax.sharding import PartitionSpec as P

BLOCK = 512
SHARPNESS = 3.5
LOG2E = math.log2(math.e)
DEAD = 1e30
MESH = pl.DeviceIdType.MESH


def kernel(
    n,
    x1_hbm,
    y1_hbm,
    h1_ref,
    w1_hbm,
    h2_ref,
    e1_hbm,
    m1_ref,
    x2_hbm,
    e2_hbm,
    m2_ref,
    out1_ref,
    out2_ref,
    x1_ref,
    y1_ref,
    w1_ref,
    e1_ref,
    x2_ref,
    e2_ref,
    states,
    offs,
    bias_ref,
    weights,
    peaks2,
    sums2,
    peak_own,
    sum_own,
    acc_own,
    send_w,
    send_s,
    recv_w,
    recv_s,
    gathered,
    far,
    near,
    vals,
    early,
    in_sem,
    st_sem,
    off_sem,
    part_send,
    part_recv,
    gat_send,
    gat_recv,
    val_sem,
):
    t = lax.axis_index("tgt")
    s = lax.axis_index("src")
    chip = t // 2
    core = lax.rem(t, 2)
    mate = jnp.bitwise_xor(chip, s)
    partner = 2 * mate + core
    sibling = 2 * chip + 1 - core
    remote = s != 0
    rows_all, width = x1_ref.shape[0], w1_ref.shape[0]
    rows = rows_all // n
    cols = y1_ref.shape[0]
    part = cols // 2
    factor = SHARPNESS / math.sqrt(x1_ref.shape[1]) * LOG2E

    def peer(i):
        return lax.rem(s + i, n)

    fetches = [
        pltpu.make_async_copy(a, b, in_sem.at[k])
        for k, (a, b) in enumerate(
            [(x1_hbm, x1_ref), (y1_hbm, y1_ref), (w1_hbm, w1_ref), (e1_hbm, e1_ref), (x2_hbm, x2_ref), (e2_hbm, e2_ref)]
        )
    ]
    for fetch in fetches:
        fetch.start()

    barrier = pltpu.get_barrier_semaphore()
    for i in range(1, n):
        pl.semaphore_signal(barrier, inc=1, device_id=(t, peer(i)), device_id_type=MESH)
    pl.semaphore_signal(barrier, inc=1, device_id=(sibling, s), device_id_type=MESH)

    @pl.when(remote)
    def _():
        pl.semaphore_signal(barrier, inc=1, device_id=(partner, s), device_id_type=MESH)

    def bias_columns(offset_row):
        full = jnp.broadcast_to(offset_row * LOG2E, (128, offset_row.shape[1]))
        return jnp.transpose(full)

    bias_ref[0] = bias_columns(h1_ref[...])
    pl.semaphore_wait(barrier, jnp.where(remote, n + 1, n))

    states_far = pltpu.make_async_remote_copy(
        x1_ref, states.at[0], st_sem.at[0], st_sem.at[1], (partner, s), MESH
    )
    states_here = pltpu.make_async_copy(x1_ref, states.at[0], st_sem.at[0])
    states_near = pltpu.make_async_remote_copy(
        states.at[0], states.at[1], st_sem.at[2], st_sem.at[3], (sibling, s), MESH
    )
    offs_far = pltpu.make_async_remote_copy(h2_ref, offs, off_sem.at[0], off_sem.at[1], (t, mate), MESH)
    offs_here = pltpu.make_async_copy(h2_ref, offs, off_sem.at[0])
    fetches[0].wait()

    @pl.when(remote)
    def _():
        states_far.start()

    @pl.when(jnp.logical_not(remote))
    def _():
        states_here.start()

    @pl.when(mate != s)
    def _():
        offs_far.start()

    @pl.when(mate == s)
    def _():
        offs_here.start()

    def softmax_part(y, x, bias, mask_ref, row_tile, col_tile):
        dots = lax.dot_general(y, x, (((1,), (1,)), ((), ())), preferred_element_type=jnp.float32)
        if rows >= 128:
            wide = jnp.concatenate([bias] * (rows // 128), axis=1)
        else:
            wide = bias[:, :rows]
        sc = dots * factor - wide
        tiles = [sc[c * BLOCK : (c + 1) * BLOCK] for c in range(sc.shape[0] // BLOCK)]
        live = [mask_ref[row_tile, col_tile + c] > 0 for c in range(len(tiles))]
        tops = [jnp.max(tile, axis=0, keepdims=True) for tile in tiles]
        peak = functools.reduce(jnp.maximum, [jnp.where(a, b, -DEAD) for a, b in zip(live, tops)])
        w = [jnp.exp2(tile - jnp.where(a, peak, DEAD)) for a, tile in zip(live, tiles)]
        total = functools.reduce(jnp.add, [jnp.sum(tile, axis=0, keepdims=True) for tile in w])
        return peak, total, jnp.concatenate([tile.astype(jnp.bfloat16) for tile in w], axis=0)

    def part_copies(d, i):
        to = (t, peer(i))
        return (
            pltpu.make_async_remote_copy(
                send_w.at[d, i], recv_w.at[d, i], part_send.at[d, 0, i], part_recv.at[d, 0, i], to, MESH
            ),
            pltpu.make_async_remote_copy(
                send_s.at[d, i], recv_s.at[d, i], part_send.at[d, 1, i], part_recv.at[d, 1, i], to, MESH
            ),
        )

    def ship(d, i, peak, total, acc):
        send_w[d, i] = acc.astype(jnp.bfloat16)
        send_s[d, i, 0:1, :] = peak
        send_s[d, i, 1:2, :] = total
        for copy in part_copies(d, i):
            copy.start()

    def keep(peak, total, acc):
        peak_own[...] = peak
        sum_own[...] = total
        acc_own[...] = acc

    def own_columns(ref):
        if rows % 128 == 0:
            return ref[:, pl.ds(pl.multiple_of(s * rows, rows), rows)].astype(jnp.float32)
        picked = jnp.zeros((width, rows), jnp.float32)
        for q in range(n):
            picked = jnp.where(s == q, ref[:, q * rows : (q + 1) * rows].astype(jnp.float32), picked)
        return picked

    def combine(d, exercise_ref):
        for i in range(1, n):
            for copy in part_copies(d, i):
                copy.wait_recv()
        peaks = [peak_own[...]] + [recv_s[d, i, 0:1, :] for i in range(1, n)]
        sums = [sum_own[...]] + [recv_s[d, i, 1:2, :] for i in range(1, n)]
        top = functools.reduce(jnp.maximum, peaks)
        shrink = jnp.exp2(peaks[0] - top)
        total = sums[0] * shrink
        acc = acc_own[...] * shrink
        for i in range(1, n):
            shrink = jnp.exp2(peaks[i] - top)
            total = total + sums[i] * shrink
            acc = acc + recv_w[d, i].astype(jnp.float32) * shrink
        return jnp.maximum(acc / total, own_columns(exercise_ref)).astype(jnp.bfloat16)

    def gather_copy(d, buffer, i, slot):
        return pltpu.make_async_remote_copy(
            buffer.at[slot], buffer.at[slot], gat_send.at[d, i], gat_recv.at[d, slot], (t, peer(i)), MESH
        )

    def first_date(i):
        q = peer(i)
        x = x1_ref[pl.ds(pl.multiple_of(q * rows, rows), rows), :]
        row_tile = (t * rows_all + q * rows) // BLOCK
        peak, total, w = softmax_part(y1_ref[...], x, bias_ref[0], m1_ref, row_tile, s * (cols // BLOCK))
        return peak, total, jnp.dot(w1_ref[...], w, preferred_element_type=jnp.float32)

    def first_step(i, carry):
        ship(0, i, *first_date(i))
        return carry

    for fetch in fetches[1:]:
        fetch.wait()
    lax.fori_loop(1, n, first_step, 0)
    keep(*first_date(0))

    gathered[s] = combine(0, e1_ref)
    for i in range(1, n):
        gather_copy(0, gathered, i, s).start()

    def far_copy(q):
        return pltpu.make_async_remote_copy(
            gathered.at[q], far.at[q], val_sem.at[0, q], val_sem.at[1, q], (partner, s), MESH
        )

    def here_copy(q):
        return pltpu.make_async_copy(gathered.at[q], far.at[q], val_sem.at[0, q])

    def near_copy(q):
        return pltpu.make_async_remote_copy(
            far.at[q], near.at[q], val_sem.at[2, q], val_sem.at[3, q], (sibling, s), MESH
        )

    def pass_on(q):
        @pl.when(remote)
        def _():
            far_copy(q).start()

        @pl.when(jnp.logical_not(remote))
        def _():
            here_copy(q).start()

    def pass_near(q):
        @pl.when(remote)
        def _():
            far_copy(q).wait_recv()

        @pl.when(jnp.logical_not(remote))
        def _():
            here_copy(q).wait()

        near_copy(q).start()

    pass_on(s)

    @pl.when(remote)
    def _():
        states_far.wait()

    @pl.when(jnp.logical_not(remote))
    def _():
        states_here.wait()

    @pl.when(mate != s)
    def _():
        offs_far.wait()

    @pl.when(mate == s)
    def _():
        offs_here.wait()

    states_near.start()
    bias_ref[1] = bias_columns(offs[...])

    def second_weights(k, low, high):
        place = core if k == 0 else 1 - core
        owner = 2 * mate + place

        def step(q, carry):
            span = pl.ds(pl.multiple_of(q * rows, rows), rows)
            row_tile = (t * rows_all + q * rows) // BLOCK
            bias = bias_ref[1, pl.ds(pl.multiple_of(place * part, part), part), :]
            peak, total, w = softmax_part(
                states[k], x2_ref[span, :], bias, m2_ref, row_tile, owner * (part // BLOCK)
            )
            weights[k, q] = w
            peaks2[k, q] = peak
            sums2[k, q] = total
            return carry

        lax.fori_loop(low, high, step, 0)

    second_weights(0, 0, n)
    states_near.wait()
    for i in range(1, n):
        gather_copy(0, gathered, i, peer(i)).wait_recv()
        pass_on(peer(i))
        second_weights(1, i - 1, i)
    pass_near(s)
    second_weights(1, n - 1, n)
    for i in range(1, n):
        pass_near(peer(i))
    for q in range(n):
        out1_ref[:, q * rows : (q + 1) * rows] = gathered[q]
        vals[0, :, q * rows : (q + 1) * rows] = far[q]
    for q in range(n):
        near_copy(q).wait_recv()
        vals[1, :, q * rows : (q + 1) * rows] = near[q]

    def second_date(i):
        q = peer(i)
        peak0, peak1 = peaks2[0, q], peaks2[1, q]
        peak = jnp.maximum(peak0, peak1)
        f0, f1 = jnp.exp2(peak0 - peak), jnp.exp2(peak1 - peak)
        total = f0 * sums2[0, q] + f1 * sums2[1, q]
        acc = f0 * jnp.dot(vals[0], weights[0, q], preferred_element_type=jnp.float32)
        acc = acc + f1 * jnp.dot(vals[1], weights[1, q], preferred_element_type=jnp.float32)
        return peak, total, acc

    def second_step(i, carry):
        ship(1, i, *second_date(i))
        return carry

    lax.fori_loop(1, n, second_step, 0)
    keep(*second_date(0))

    early[s] = combine(1, e2_ref)
    for i in range(1, n):
        gather_copy(1, early, i, s).start()
    for i in range(1, n):
        gather_copy(1, early, i, peer(i)).wait_recv()
    for q in range(n):
        out2_ref[:, q * rows : (q + 1) * rows] = early[q]

    for d in range(2):
        for i in range(1, n):
            for copy in part_copies(d, i):
                copy.wait_send()
            gather_copy(d, gathered if d == 0 else early, i, s).wait_send()
    for q in range(n):
        near_copy(q).wait_send()

        @pl.when(remote)
        def _():
            far_copy(q).wait_send()


def per_device(n, states_late, offset_late, values_late, states_mid, offset_mid, exercise_mid, mask_mid,
               states_early, exercise_early, mask_early):
    rows_all, factors = states_mid.shape
    cols, width = values_late.shape
    rows = rows_all // n
    part = cols // 2
    bf16, f32 = jnp.bfloat16, jnp.float32
    vmem = pl.BlockSpec(memory_space=pltpu.VMEM)
    smem = pl.BlockSpec(memory_space=pltpu.SMEM)
    hbm = pl.BlockSpec(memory_space=pltpu.HBM)
    pairs = 2 * rows_all * cols
    call = pl.pallas_call(
        functools.partial(kernel, n),
        out_shape=(
            jax.ShapeDtypeStruct((width, rows_all), bf16),
            jax.ShapeDtypeStruct((width, rows_all), bf16),
        ),
        in_specs=[hbm, hbm, vmem, hbm, vmem, hbm, smem, hbm, hbm, smem],
        out_specs=(vmem, vmem),
        scratch_shapes=[
            pltpu.VMEM((rows_all, factors), bf16),
            pltpu.VMEM((cols, factors), bf16),
            pltpu.VMEM((width, cols), bf16),
            pltpu.VMEM((width, rows_all), bf16),
            pltpu.VMEM((rows_all, factors), bf16),
            pltpu.VMEM((width, rows_all), bf16),
            pltpu.VMEM((2, rows_all, factors), bf16),
            pltpu.VMEM((1, cols), f32),
            pltpu.VMEM((2, cols, 128), f32),
            pltpu.VMEM((2, n, part, rows), bf16),
            pltpu.VMEM((2, n, 1, rows), f32),
            pltpu.VMEM((2, n, 1, rows), f32),
            pltpu.VMEM((1, rows), f32),
            pltpu.VMEM((1, rows), f32),
            pltpu.VMEM((width, rows), f32),
            pltpu.VMEM((2, n, width, rows), bf16),
            pltpu.VMEM((2, n, 2, rows), f32),
            pltpu.VMEM((2, n, width, rows), bf16),
            pltpu.VMEM((2, n, 2, rows), f32),
            pltpu.VMEM((n, width, rows), bf16),
            pltpu.VMEM((n, width, rows), bf16),
            pltpu.VMEM((n, width, rows), bf16),
            pltpu.VMEM((2, width, part), bf16),
            pltpu.VMEM((n, width, rows), bf16),
            pltpu.SemaphoreType.DMA((6,)),
            pltpu.SemaphoreType.DMA((4,)),
            pltpu.SemaphoreType.DMA((2,)),
            pltpu.SemaphoreType.DMA((2, 2, n)),
            pltpu.SemaphoreType.DMA((2, 2, n)),
            pltpu.SemaphoreType.DMA((2, n)),
            pltpu.SemaphoreType.DMA((2, n)),
            pltpu.SemaphoreType.DMA((4, n)),
        ],
        compiler_params=pltpu.CompilerParams(
            collective_id=0, has_side_effects=True, vmem_limit_bytes=62 * 1024 * 1024
        ),
        cost_estimate=pl.CostEstimate(
            flops=2 * pairs * (factors + width), bytes_accessed=4 * 1024 * 1024, transcendentals=pairs
        ),
    )
    value_mid, value_early = call(
        states_mid,
        states_late,
        offset_late.astype(f32).reshape(1, cols),
        values_late.T,
        offset_mid.astype(f32).reshape(1, cols),
        exercise_mid.T,
        mask_mid,
        states_early,
        exercise_early.T,
        mask_early,
    )
    return value_mid.T, value_early.T


def solution(mesh):
    in_specs = (
        P("src", None),
        P("src"),
        P("src", None),
        P("tgt", None),
        P("src"),
        P("tgt", None),
        P(),
        P("tgt", None),
        P("tgt", None),
        P(),
    )
    out_specs = (P("tgt", None), P("tgt", None))
    return jax.shard_map(
        functools.partial(per_device, mesh.shape["src"]),
        mesh=mesh,
        in_specs=in_specs,
        out_specs=out_specs,
        check_vma=False,
    )
```

```python
import functools
import math

import jax
import jax.numpy as jnp
from jax import lax
from jax.experimental import pallas as pl
from jax.experimental.pallas import tpu as pltpu
from jax.sharding import PartitionSpec as P

BLOCK = 512
SHARPNESS = 3.5
LOG2E = math.log2(math.e)
DEAD = 1e30
MESH = pl.DeviceIdType.MESH


def kernel(
    n,
    x1_hbm,
    y1_hbm,
    h_ref,
    w1_hbm,
    e1_hbm,
    m1_ref,
    x2_hbm,
    e2_hbm,
    m2_ref,
    out1_ref,
    out2_ref,
    x1_ref,
    y1_ref,
    w1_ref,
    e1_ref,
    x2_ref,
    e2_ref,
    states,
    offs,
    bias_ref,
    weights,
    peaks2,
    sums2,
    peak_own,
    sum_own,
    acc_own,
    send_w,
    send_s,
    recv_w,
    recv_s,
    gathered,
    far,
    near,
    vals,
    early,
    in_sem,
    st_sem,
    off_sem,
    part_send,
    part_recv,
    gat_send,
    gat_recv,
    val_sem,
):
    t = lax.axis_index("tgt")
    s = lax.axis_index("src")
    chip = t // 2
    core = lax.rem(t, 2)
    mate = jnp.bitwise_xor(chip, s)
    partner = 2 * mate + core
    sibling = 2 * chip + 1 - core
    remote = s != 0
    rows_all, width = x1_ref.shape[0], w1_ref.shape[0]
    rows = rows_all // n
    cols = y1_ref.shape[0]
    part = cols // 2
    factor = SHARPNESS / math.sqrt(x1_ref.shape[1]) * LOG2E

    def peer(i):
        return lax.rem(s + i, n)

    fetches = [
        pltpu.make_async_copy(a, b, in_sem.at[k])
        for k, (a, b) in enumerate(
            [(x1_hbm, x1_ref), (y1_hbm, y1_ref), (w1_hbm, w1_ref), (e1_hbm, e1_ref), (x2_hbm, x2_ref), (e2_hbm, e2_ref)]
        )
    ]
    for fetch in fetches:
        fetch.start()

    barrier = pltpu.get_barrier_semaphore()
    for i in range(1, n):
        pl.semaphore_signal(barrier, inc=1, device_id=(t, peer(i)), device_id_type=MESH)
    pl.semaphore_signal(barrier, inc=1, device_id=(sibling, s), device_id_type=MESH)

    @pl.when(remote)
    def _():
        pl.semaphore_signal(barrier, inc=1, device_id=(partner, s), device_id_type=MESH)

    def bias_columns(offset_row):
        full = jnp.broadcast_to(offset_row * LOG2E, (128, offset_row.shape[1]))
        return jnp.transpose(full)

    bias_ref[0] = bias_columns(h_ref[0])
    pl.semaphore_wait(barrier, jnp.where(remote, n + 1, n))

    states_far = pltpu.make_async_remote_copy(
        x1_ref, states.at[0], st_sem.at[0], st_sem.at[1], (partner, s), MESH
    )
    states_here = pltpu.make_async_copy(x1_ref, states.at[0], st_sem.at[0])
    states_near = pltpu.make_async_remote_copy(
        states.at[0], states.at[1], st_sem.at[2], st_sem.at[3], (sibling, s), MESH
    )
    offs_far = pltpu.make_async_remote_copy(h_ref.at[1], offs, off_sem.at[0], off_sem.at[1], (t, mate), MESH)
    offs_here = pltpu.make_async_copy(h_ref.at[1], offs, off_sem.at[0])
    fetches[0].wait()

    @pl.when(remote)
    def _():
        states_far.start()

    @pl.when(jnp.logical_not(remote))
    def _():
        states_here.start()

    @pl.when(mate != s)
    def _():
        offs_far.start()

    @pl.when(mate == s)
    def _():
        offs_here.start()

    def softmax_part(y, x, bias, mask_ref, row_tile, col_tile):
        dots = lax.dot_general(y, x, (((1,), (1,)), ((), ())), preferred_element_type=jnp.float32)
        if rows >= 128:
            wide = jnp.concatenate([bias] * (rows // 128), axis=1)
        else:
            wide = bias[:, :rows]
        sc = dots * factor - wide
        tiles = [sc[c * BLOCK : (c + 1) * BLOCK] for c in range(sc.shape[0] // BLOCK)]
        live = [mask_ref[row_tile, col_tile + c] > 0 for c in range(len(tiles))]
        tops = [jnp.max(tile, axis=0, keepdims=True) for tile in tiles]
        peak = functools.reduce(jnp.maximum, [jnp.where(a, b, -DEAD) for a, b in zip(live, tops)])
        w = [jnp.exp2(tile - jnp.where(a, peak, DEAD)) for a, tile in zip(live, tiles)]
        total = functools.reduce(jnp.add, [jnp.sum(tile, axis=0, keepdims=True) for tile in w])
        return peak, total, jnp.concatenate([tile.astype(jnp.bfloat16) for tile in w], axis=0)

    def part_copies(d, i):
        to = (t, peer(i))
        return (
            pltpu.make_async_remote_copy(
                send_w.at[d, i], recv_w.at[d, i], part_send.at[d, 0, i], part_recv.at[d, 0, i], to, MESH
            ),
            pltpu.make_async_remote_copy(
                send_s.at[d, i], recv_s.at[d, i], part_send.at[d, 1, i], part_recv.at[d, 1, i], to, MESH
            ),
        )

    def ship(d, i, peak, total, acc):
        send_w[d, i] = acc.astype(jnp.bfloat16)
        send_s[d, i, 0:1, :] = peak
        send_s[d, i, 1:2, :] = total
        for copy in part_copies(d, i):
            copy.start()

    def keep(peak, total, acc):
        peak_own[...] = peak
        sum_own[...] = total
        acc_own[...] = acc

    def own_columns(ref):
        if rows % 128 == 0:
            return ref[:, pl.ds(pl.multiple_of(s * rows, rows), rows)].astype(jnp.float32)
        picked = jnp.zeros((width, rows), jnp.float32)
        for q in range(n):
            picked = jnp.where(s == q, ref[:, q * rows : (q + 1) * rows].astype(jnp.float32), picked)
        return picked

    def combine(d, exercise_ref):
        for i in range(1, n):
            for copy in part_copies(d, i):
                copy.wait_recv()
        peaks = [peak_own[...]] + [recv_s[d, i, 0:1, :] for i in range(1, n)]
        sums = [sum_own[...]] + [recv_s[d, i, 1:2, :] for i in range(1, n)]
        top = functools.reduce(jnp.maximum, peaks)
        shrink = jnp.exp2(peaks[0] - top)
        total = sums[0] * shrink
        acc = acc_own[...] * shrink
        for i in range(1, n):
            shrink = jnp.exp2(peaks[i] - top)
            total = total + sums[i] * shrink
            acc = acc + recv_w[d, i].astype(jnp.float32) * shrink
        return jnp.maximum(acc / total, own_columns(exercise_ref)).astype(jnp.bfloat16)

    def gather_copy(d, buffer, i, slot):
        return pltpu.make_async_remote_copy(
            buffer.at[slot], buffer.at[slot], gat_send.at[d, i], gat_recv.at[d, slot], (t, peer(i)), MESH
        )

    def first_date(i):
        q = peer(i)
        x = x1_ref[pl.ds(pl.multiple_of(q * rows, rows), rows), :]
        row_tile = (t * rows_all + q * rows) // BLOCK
        peak, total, w = softmax_part(y1_ref[...], x, bias_ref[0], m1_ref, row_tile, s * (cols // BLOCK))
        return peak, total, jnp.dot(w1_ref[...], w, preferred_element_type=jnp.float32)

    def first_step(i, carry):
        ship(0, i, *first_date(i))
        return carry

    fetches[1].wait()
    fetches[2].wait()
    lax.fori_loop(1, n, first_step, 0)
    keep(*first_date(0))

    for fetch in fetches[3:]:
        fetch.wait()
    gathered[s] = combine(0, e1_ref)
    for i in range(1, n):
        gather_copy(0, gathered, i, s).start()

    def far_copy(q):
        return pltpu.make_async_remote_copy(
            gathered.at[q], far.at[q], val_sem.at[0, q], val_sem.at[1, q], (partner, s), MESH
        )

    def here_copy(q):
        return pltpu.make_async_copy(gathered.at[q], far.at[q], val_sem.at[0, q])

    def near_copy(q):
        return pltpu.make_async_remote_copy(
            far.at[q], near.at[q], val_sem.at[2, q], val_sem.at[3, q], (sibling, s), MESH
        )

    def pass_on(q):
        @pl.when(remote)
        def _():
            far_copy(q).start()

        @pl.when(jnp.logical_not(remote))
        def _():
            here_copy(q).start()

    def pass_near(q):
        @pl.when(remote)
        def _():
            far_copy(q).wait_recv()

        @pl.when(jnp.logical_not(remote))
        def _():
            here_copy(q).wait()

        near_copy(q).start()

    pass_on(s)

    @pl.when(remote)
    def _():
        states_far.wait()

    @pl.when(jnp.logical_not(remote))
    def _():
        states_here.wait()

    @pl.when(mate != s)
    def _():
        offs_far.wait()

    @pl.when(mate == s)
    def _():
        offs_here.wait()

    states_near.start()
    bias_ref[1] = bias_columns(offs[...])

    def second_weights(k, low, high):
        place = core if k == 0 else 1 - core
        owner = 2 * mate + place

        def step(q, carry):
            span = pl.ds(pl.multiple_of(q * rows, rows), rows)
            row_tile = (t * rows_all + q * rows) // BLOCK
            bias = bias_ref[1, pl.ds(pl.multiple_of(place * part, part), part), :]
            peak, total, w = softmax_part(
                states[k], x2_ref[span, :], bias, m2_ref, row_tile, owner * (part // BLOCK)
            )
            weights[k, q] = w
            peaks2[k, q] = peak
            sums2[k, q] = total
            return carry

        lax.fori_loop(low, high, step, 0)

    second_weights(0, 0, n)
    states_near.wait()
    for i in range(1, n):
        gather_copy(0, gathered, i, peer(i)).wait_recv()
        pass_on(peer(i))
        second_weights(1, i - 1, i)
    pass_near(s)
    second_weights(1, n - 1, n)
    for i in range(1, n):
        pass_near(peer(i))
    for q in range(n):
        out1_ref[:, q * rows : (q + 1) * rows] = gathered[q]
        vals[0, :, q * rows : (q + 1) * rows] = far[q]
    for q in range(n):
        near_copy(q).wait_recv()
        vals[1, :, q * rows : (q + 1) * rows] = near[q]

    def second_date(i):
        q = peer(i)
        peak0, peak1 = peaks2[0, q], peaks2[1, q]
        peak = jnp.maximum(peak0, peak1)
        f0, f1 = jnp.exp2(peak0 - peak), jnp.exp2(peak1 - peak)
        total = f0 * sums2[0, q] + f1 * sums2[1, q]
        acc = f0 * jnp.dot(vals[0], weights[0, q], preferred_element_type=jnp.float32)
        acc = acc + f1 * jnp.dot(vals[1], weights[1, q], preferred_element_type=jnp.float32)
        return peak, total, acc

    def second_step(i, carry):
        ship(1, i, *second_date(i))
        return carry

    lax.fori_loop(1, n, second_step, 0)
    keep(*second_date(0))

    early[s] = combine(1, e2_ref)
    for i in range(1, n):
        gather_copy(1, early, i, s).start()
    for i in range(1, n):
        gather_copy(1, early, i, peer(i)).wait_recv()
    for q in range(n):
        out2_ref[:, q * rows : (q + 1) * rows] = early[q]

    for d in range(2):
        for i in range(1, n):
            for copy in part_copies(d, i):
                copy.wait_send()
            gather_copy(d, gathered if d == 0 else early, i, s).wait_send()
    for q in range(n):
        near_copy(q).wait_send()

        @pl.when(remote)
        def _():
            far_copy(q).wait_send()


def per_device(n, states_late, offset_late, values_late, states_mid, offset_mid, exercise_mid, mask_mid,
               states_early, exercise_early, mask_early):
    rows_all, factors = states_mid.shape
    cols, width = values_late.shape
    rows = rows_all // n
    part = cols // 2
    bf16, f32 = jnp.bfloat16, jnp.float32
    vmem = pl.BlockSpec(memory_space=pltpu.VMEM)
    smem = pl.BlockSpec(memory_space=pltpu.SMEM)
    hbm = pl.BlockSpec(memory_space=pltpu.HBM)
    pairs = 2 * rows_all * cols
    call = pl.pallas_call(
        functools.partial(kernel, n),
        out_shape=(
            jax.ShapeDtypeStruct((width, rows_all), bf16),
            jax.ShapeDtypeStruct((width, rows_all), bf16),
        ),
        in_specs=[hbm, hbm, vmem, hbm, hbm, smem, hbm, hbm, smem],
        out_specs=(vmem, vmem),
        scratch_shapes=[
            pltpu.VMEM((rows_all, factors), bf16),
            pltpu.VMEM((cols, factors), bf16),
            pltpu.VMEM((width, cols), bf16),
            pltpu.VMEM((width, rows_all), bf16),
            pltpu.VMEM((rows_all, factors), bf16),
            pltpu.VMEM((width, rows_all), bf16),
            pltpu.VMEM((2, rows_all, factors), bf16),
            pltpu.VMEM((1, cols), f32),
            pltpu.VMEM((2, cols, 128), f32),
            pltpu.VMEM((2, n, part, rows), bf16),
            pltpu.VMEM((2, n, 1, rows), f32),
            pltpu.VMEM((2, n, 1, rows), f32),
            pltpu.VMEM((1, rows), f32),
            pltpu.VMEM((1, rows), f32),
            pltpu.VMEM((width, rows), f32),
            pltpu.VMEM((2, n, width, rows), bf16),
            pltpu.VMEM((2, n, 2, rows), f32),
            pltpu.VMEM((2, n, width, rows), bf16),
            pltpu.VMEM((2, n, 2, rows), f32),
            pltpu.VMEM((n, width, rows), bf16),
            pltpu.VMEM((n, width, rows), bf16),
            pltpu.VMEM((n, width, rows), bf16),
            pltpu.VMEM((2, width, part), bf16),
            pltpu.VMEM((n, width, rows), bf16),
            pltpu.SemaphoreType.DMA((6,)),
            pltpu.SemaphoreType.DMA((4,)),
            pltpu.SemaphoreType.DMA((2,)),
            pltpu.SemaphoreType.DMA((2, 2, n)),
            pltpu.SemaphoreType.DMA((2, 2, n)),
            pltpu.SemaphoreType.DMA((2, n)),
            pltpu.SemaphoreType.DMA((2, n)),
            pltpu.SemaphoreType.DMA((4, n)),
        ],
        compiler_params=pltpu.CompilerParams(
            collective_id=0, has_side_effects=True, vmem_limit_bytes=62 * 1024 * 1024
        ),
        cost_estimate=pl.CostEstimate(
            flops=2 * pairs * (factors + width), bytes_accessed=4 * 1024 * 1024, transcendentals=pairs
        ),
    )
    value_mid, value_early = call(
        states_mid,
        states_late,
        jnp.stack([offset_late, offset_mid]).astype(f32).reshape(2, 1, cols),
        values_late.T,
        exercise_mid.T,
        mask_mid,
        states_early,
        exercise_early.T,
        mask_early,
    )
    return value_mid.T, value_early.T


def solution(mesh):
    in_specs = (
        P("src", None),
        P("src"),
        P("src", None),
        P("tgt", None),
        P("src"),
        P("tgt", None),
        P(),
        P("tgt", None),
        P("tgt", None),
        P(),
    )
    out_specs = (P("tgt", None), P("tgt", None))
    return jax.shard_map(
        functools.partial(per_device, mesh.shape["src"]),
        mesh=mesh,
        in_specs=in_specs,
        out_specs=out_specs,
        check_vma=False,
    )
```

```python
import functools
import math

import jax
import jax.numpy as jnp
from jax import lax
from jax.experimental import pallas as pl
from jax.experimental.pallas import tpu as pltpu
from jax.sharding import PartitionSpec as P

BLOCK = 512
SHARPNESS = 3.5
LOG2E = math.log2(math.e)
DEAD = 1e30
MESH = pl.DeviceIdType.MESH


def kernel(
    n,
    x1_hbm,
    y1_hbm,
    h1_ref,
    w1_hbm,
    h2_ref,
    e1_hbm,
    m1_ref,
    x2_hbm,
    e2_hbm,
    m2_ref,
    out1_ref,
    out2_ref,
    x1_ref,
    y1_ref,
    w1_ref,
    e1_ref,
    x2_ref,
    e2_ref,
    states,
    offs,
    bias_ref,
    weights,
    peaks2,
    sums2,
    peak_own,
    sum_own,
    acc_own,
    send_w,
    send_s,
    recv_w,
    recv_s,
    gathered,
    far,
    near,
    vals,
    early,
    in_sem,
    st_sem,
    off_sem,
    part_send,
    part_recv,
    gat_send,
    gat_recv,
    val_sem,
):
    t = lax.axis_index("tgt")
    s = lax.axis_index("src")
    chip = t // 2
    core = lax.rem(t, 2)
    mate = jnp.bitwise_xor(chip, s)
    partner = 2 * mate + core
    sibling = 2 * chip + 1 - core
    remote = s != 0
    rows_all, width = x1_ref.shape[0], w1_ref.shape[0]
    rows = rows_all // n
    cols = y1_ref.shape[0]
    part = cols // 2
    factor = SHARPNESS / math.sqrt(x1_ref.shape[1]) * LOG2E

    def peer(i):
        return lax.rem(s + i, n)

    fetches = [
        pltpu.make_async_copy(a, b, in_sem.at[k])
        for k, (a, b) in enumerate(
            [(x1_hbm, x1_ref), (y1_hbm, y1_ref), (w1_hbm, w1_ref), (e1_hbm, e1_ref), (x2_hbm, x2_ref), (e2_hbm, e2_ref)]
        )
    ]
    for fetch in fetches:
        fetch.start()

    barrier = pltpu.get_barrier_semaphore()
    for i in range(1, n):
        pl.semaphore_signal(barrier, inc=1, device_id=(t, peer(i)), device_id_type=MESH)
    pl.semaphore_signal(barrier, inc=1, device_id=(sibling, s), device_id_type=MESH)

    @pl.when(remote)
    def _():
        pl.semaphore_signal(barrier, inc=1, device_id=(partner, s), device_id_type=MESH)

    def bias_columns(offset_row):
        full = jnp.broadcast_to(offset_row * LOG2E, (128, offset_row.shape[1]))
        return jnp.transpose(full)

    bias_ref[0] = bias_columns(h1_ref[...])
    pl.semaphore_wait(barrier, jnp.where(remote, n + 1, n))

    states_far = pltpu.make_async_remote_copy(
        x1_ref, states.at[0], st_sem.at[0], st_sem.at[1], (partner, s), MESH
    )
    states_here = pltpu.make_async_copy(x1_ref, states.at[0], st_sem.at[0])
    states_near = pltpu.make_async_remote_copy(
        states.at[0], states.at[1], st_sem.at[2], st_sem.at[3], (sibling, s), MESH
    )
    offs_far = pltpu.make_async_remote_copy(h2_ref, offs, off_sem.at[0], off_sem.at[1], (t, mate), MESH)
    offs_here = pltpu.make_async_copy(h2_ref, offs, off_sem.at[0])
    fetches[0].wait()

    @pl.when(remote)
    def _():
        states_far.start()

    @pl.when(jnp.logical_not(remote))
    def _():
        states_here.start()

    @pl.when(mate != s)
    def _():
        offs_far.start()

    @pl.when(mate == s)
    def _():
        offs_here.start()

    def softmax_part(y, x, bias, mask_ref, row_tile, col_tile):
        dots = lax.dot_general(y, x, (((1,), (1,)), ((), ())), preferred_element_type=jnp.float32)
        if rows >= 128:
            wide = jnp.concatenate([bias] * (rows // 128), axis=1)
        else:
            wide = bias[:, :rows]
        sc = dots * factor - wide
        tiles = [sc[c * BLOCK : (c + 1) * BLOCK] for c in range(sc.shape[0] // BLOCK)]
        live = [mask_ref[row_tile, col_tile + c] > 0 for c in range(len(tiles))]
        tops = [jnp.max(tile, axis=0, keepdims=True) for tile in tiles]
        peak = functools.reduce(jnp.maximum, [jnp.where(a, b, -DEAD) for a, b in zip(live, tops)])
        w = [jnp.exp2(tile - jnp.where(a, peak, DEAD)) for a, tile in zip(live, tiles)]
        total = functools.reduce(jnp.add, [jnp.sum(tile, axis=0, keepdims=True) for tile in w])
        return peak, total, jnp.concatenate([tile.astype(jnp.bfloat16) for tile in w], axis=0)

    def part_copies(d, i):
        to = (t, peer(i))
        return (
            pltpu.make_async_remote_copy(
                send_w.at[d, i], recv_w.at[d, i], part_send.at[d, 0, i], part_recv.at[d, 0, i], to, MESH
            ),
            pltpu.make_async_remote_copy(
                send_s.at[d, i], recv_s.at[d, i], part_send.at[d, 1, i], part_recv.at[d, 1, i], to, MESH
            ),
        )

    def ship(d, i, peak, total, acc):
        send_w[d, i] = acc.astype(jnp.bfloat16)
        send_s[d, i, 0:1, :] = peak
        send_s[d, i, 1:2, :] = total
        for copy in part_copies(d, i):
            copy.start()

    def keep(peak, total, acc):
        peak_own[...] = peak
        sum_own[...] = total
        acc_own[...] = acc

    def own_columns(ref):
        if rows % 128 == 0:
            return ref[:, pl.ds(pl.multiple_of(s * rows, rows), rows)].astype(jnp.float32)
        picked = jnp.zeros((width, rows), jnp.float32)
        for q in range(n):
            picked = jnp.where(s == q, ref[:, q * rows : (q + 1) * rows].astype(jnp.float32), picked)
        return picked

    def combine(d, exercise_ref):
        for i in range(1, n):
            for copy in part_copies(d, i):
                copy.wait_recv()
        peaks = [peak_own[...]] + [recv_s[d, i, 0:1, :] for i in range(1, n)]
        sums = [sum_own[...]] + [recv_s[d, i, 1:2, :] for i in range(1, n)]
        top = functools.reduce(jnp.maximum, peaks)
        shrink = jnp.exp2(peaks[0] - top)
        total = sums[0] * shrink
        acc = acc_own[...] * shrink
        for i in range(1, n):
            shrink = jnp.exp2(peaks[i] - top)
            total = total + sums[i] * shrink
            acc = acc + recv_w[d, i].astype(jnp.float32) * shrink
        return jnp.maximum(acc / total, own_columns(exercise_ref)).astype(jnp.bfloat16)

    def gather_copy(d, buffer, i, slot):
        return pltpu.make_async_remote_copy(
            buffer.at[slot], buffer.at[slot], gat_send.at[d, i], gat_recv.at[d, slot], (t, peer(i)), MESH
        )

    def first_date(i):
        q = peer(i)
        x = x1_ref[pl.ds(pl.multiple_of(q * rows, rows), rows), :]
        row_tile = (t * rows_all + q * rows) // BLOCK
        peak, total, w = softmax_part(y1_ref[...], x, bias_ref[0], m1_ref, row_tile, s * (cols // BLOCK))
        return peak, total, jnp.dot(w1_ref[...], w, preferred_element_type=jnp.float32)

    def first_step(i, carry):
        ship(0, i, *first_date(i))
        return carry

    for fetch in fetches[1:]:
        fetch.wait()
    lax.fori_loop(1, n, first_step, 0)
    keep(*first_date(0))

    gathered[s] = combine(0, e1_ref)
    for i in range(1, n):
        gather_copy(0, gathered, i, s).start()

    def far_copy(q):
        return pltpu.make_async_remote_copy(
            gathered.at[q], far.at[q], val_sem.at[0, q], val_sem.at[1, q], (partner, s), MESH
        )

    def here_copy(q):
        return pltpu.make_async_copy(gathered.at[q], far.at[q], val_sem.at[0, q])

    def near_copy(q):
        return pltpu.make_async_remote_copy(
            far.at[q], near.at[q], val_sem.at[2, q], val_sem.at[3, q], (sibling, s), MESH
        )

    def pass_on(q):
        @pl.when(remote)
        def _():
            far_copy(q).start()

        @pl.when(jnp.logical_not(remote))
        def _():
            here_copy(q).start()

    def pass_near(q):
        @pl.when(remote)
        def _():
            far_copy(q).wait_recv()

        @pl.when(jnp.logical_not(remote))
        def _():
            here_copy(q).wait()

        near_copy(q).start()

    pass_on(s)

    @pl.when(remote)
    def _():
        states_far.wait()

    @pl.when(jnp.logical_not(remote))
    def _():
        states_here.wait()

    @pl.when(mate != s)
    def _():
        offs_far.wait()

    @pl.when(mate == s)
    def _():
        offs_here.wait()

    states_near.start()
    bias_ref[1] = bias_columns(offs[...])

    def second_weights(k, low, high):
        place = core if k == 0 else 1 - core
        owner = 2 * mate + place

        def step(q, carry):
            span = pl.ds(pl.multiple_of(q * rows, rows), rows)
            row_tile = (t * rows_all + q * rows) // BLOCK
            bias = bias_ref[1, pl.ds(pl.multiple_of(place * part, part), part), :]
            peak, total, w = softmax_part(
                states[k], x2_ref[span, :], bias, m2_ref, row_tile, owner * (part // BLOCK)
            )
            weights[k, q] = w
            peaks2[k, q] = peak
            sums2[k, q] = total
            return carry

        lax.fori_loop(low, high, step, 0)

    second_weights(0, 0, n)
    states_near.wait()
    for i in range(1, n):
        gather_copy(0, gathered, i, peer(i)).wait_recv()
        pass_on(peer(i))
        second_weights(1, i - 1, i)
    pass_near(s)
    second_weights(1, n - 1, n)
    for i in range(1, n):
        pass_near(peer(i))
    for q in range(n):
        out1_ref[:, q * rows : (q + 1) * rows] = gathered[q]
        vals[0, :, q * rows : (q + 1) * rows] = far[q]
    for q in range(n):
        near_copy(q).wait_recv()
        vals[1, :, q * rows : (q + 1) * rows] = near[q]

    def second_date(i):
        q = peer(i)
        peak0, peak1 = peaks2[0, q], peaks2[1, q]
        peak = jnp.maximum(peak0, peak1)
        f0, f1 = jnp.exp2(peak0 - peak), jnp.exp2(peak1 - peak)
        total = f0 * sums2[0, q] + f1 * sums2[1, q]
        acc = f0 * jnp.dot(vals[0], weights[0, q], preferred_element_type=jnp.float32)
        acc = acc + f1 * jnp.dot(vals[1], weights[1, q], preferred_element_type=jnp.float32)
        return peak, total, acc

    def second_step(i, carry):
        ship(1, i, *second_date(i))
        return carry

    lax.fori_loop(1, n, second_step, 0, unroll=n <= 4)
    keep(*second_date(0))

    early[s] = combine(1, e2_ref)
    for i in range(1, n):
        gather_copy(1, early, i, s).start()
    for i in range(1, n):
        gather_copy(1, early, i, peer(i)).wait_recv()
    for q in range(n):
        out2_ref[:, q * rows : (q + 1) * rows] = early[q]

    for d in range(2):
        for i in range(1, n):
            for copy in part_copies(d, i):
                copy.wait_send()
            gather_copy(d, gathered if d == 0 else early, i, s).wait_send()
    for q in range(n):
        near_copy(q).wait_send()

        @pl.when(remote)
        def _():
            far_copy(q).wait_send()


def per_device(n, states_late, offset_late, values_late, states_mid, offset_mid, exercise_mid, mask_mid,
               states_early, exercise_early, mask_early):
    rows_all, factors = states_mid.shape
    cols, width = values_late.shape
    rows = rows_all // n
    part = cols // 2
    bf16, f32 = jnp.bfloat16, jnp.float32
    vmem = pl.BlockSpec(memory_space=pltpu.VMEM)
    smem = pl.BlockSpec(memory_space=pltpu.SMEM)
    hbm = pl.BlockSpec(memory_space=pltpu.HBM)
    pairs = 2 * rows_all * cols
    call = pl.pallas_call(
        functools.partial(kernel, n),
        out_shape=(
            jax.ShapeDtypeStruct((width, rows_all), bf16),
            jax.ShapeDtypeStruct((width, rows_all), bf16),
        ),
        in_specs=[hbm, hbm, vmem, hbm, vmem, hbm, smem, hbm, hbm, smem],
        out_specs=(vmem, vmem),
        scratch_shapes=[
            pltpu.VMEM((rows_all, factors), bf16),
            pltpu.VMEM((cols, factors), bf16),
            pltpu.VMEM((width, cols), bf16),
            pltpu.VMEM((width, rows_all), bf16),
            pltpu.VMEM((rows_all, factors), bf16),
            pltpu.VMEM((width, rows_all), bf16),
            pltpu.VMEM((2, rows_all, factors), bf16),
            pltpu.VMEM((1, cols), f32),
            pltpu.VMEM((2, cols, 128), f32),
            pltpu.VMEM((2, n, part, rows), bf16),
            pltpu.VMEM((2, n, 1, rows), f32),
            pltpu.VMEM((2, n, 1, rows), f32),
            pltpu.VMEM((1, rows), f32),
            pltpu.VMEM((1, rows), f32),
            pltpu.VMEM((width, rows), f32),
            pltpu.VMEM((2, n, width, rows), bf16),
            pltpu.VMEM((2, n, 2, rows), f32),
            pltpu.VMEM((2, n, width, rows), bf16),
            pltpu.VMEM((2, n, 2, rows), f32),
            pltpu.VMEM((n, width, rows), bf16),
            pltpu.VMEM((n, width, rows), bf16),
            pltpu.VMEM((n, width, rows), bf16),
            pltpu.VMEM((2, width, part), bf16),
            pltpu.VMEM((n, width, rows), bf16),
            pltpu.SemaphoreType.DMA((6,)),
            pltpu.SemaphoreType.DMA((4,)),
            pltpu.SemaphoreType.DMA((2,)),
            pltpu.SemaphoreType.DMA((2, 2, n)),
            pltpu.SemaphoreType.DMA((2, 2, n)),
            pltpu.SemaphoreType.DMA((2, n)),
            pltpu.SemaphoreType.DMA((2, n)),
            pltpu.SemaphoreType.DMA((4, n)),
        ],
        compiler_params=pltpu.CompilerParams(
            collective_id=0, has_side_effects=True, vmem_limit_bytes=62 * 1024 * 1024
        ),
        cost_estimate=pl.CostEstimate(
            flops=2 * pairs * (factors + width), bytes_accessed=4 * 1024 * 1024, transcendentals=pairs
        ),
    )
    value_mid, value_early = call(
        states_mid,
        states_late,
        offset_late.astype(f32).reshape(1, cols),
        values_late.T,
        offset_mid.astype(f32).reshape(1, cols),
        exercise_mid.T,
        mask_mid,
        states_early,
        exercise_early.T,
        mask_early,
    )
    return value_mid.T, value_early.T


def solution(mesh):
    in_specs = (
        P("src", None),
        P("src"),
        P("src", None),
        P("tgt", None),
        P("src"),
        P("tgt", None),
        P(),
        P("tgt", None),
        P("tgt", None),
        P(),
    )
    out_specs = (P("tgt", None), P("tgt", None))
    return jax.shard_map(
        functools.partial(per_device, mesh.shape["src"]),
        mesh=mesh,
        in_specs=in_specs,
        out_specs=out_specs,
        check_vma=False,
    )
```
